256 devices in a mesh: inst: 32 (over z_lo, y, x), tp: 8 (over z_hi, core).
Axes of the slice: x: 4, y: 4, z: 8 (z_hi: 4, z_lo: 2; z = z_hi * 2 + z_lo), core: 2. Of those that a mesh axis runs over, the one named last changes fastest.
Arguments:
- query_one: bfloat16 [1024, 64, 128], P('inst', 'tp'), may hold values from -32 to 32
- key_one: bfloat16 [1024, 8, 128], P('inst', 'tp'), may hold values from -6 to 6
- value_one: bfloat16 [1024, 8, 128], P('inst', 'tp'), may hold values from -6 to 6
- key_pages: bfloat16 [4096, 8, 64, 128], P('inst', 'tp'), may hold values from -32 to 32
- value_pages: bfloat16 [4096, 8, 64, 128], P('inst', 'tp'), may hold values from -6 to 6
- page_table: int32 [1024, 4], P('inst'), may hold values from 0 to 127, as said below
- lengths: int32 [1024], P('inst'), may hold values from 8 to 254, as said below
- dest_instance: int32 [1024], P('inst'), may hold values from 0 to 31, as said below
- dest_slot: int32 [1024], P('inst'), may hold values from 0 to 31, as said below
- query_two: bfloat16 [1024, 64, 128], P('inst', 'tp'), may hold values from -32 to 32
- key_two: bfloat16 [1024, 8, 128], P('inst', 'tp'), may hold values from -6 to 6
- value_two: bfloat16 [1024, 8, 128], P('inst', 'tp'), may hold values from -6 to 6
- out_weight: bfloat16 [8192, 4096], P('tp'), may hold values from -0.1875 to 0.1875
Outputs:
- out_one: bfloat16 [1024, 4096], P('inst')
- out_two: bfloat16 [1024, 4096], P('inst')
- key_cache: bfloat16 [4096, 8, 64, 128], P('inst', 'tp')
- value_cache: bfloat16 [4096, 8, 64, 128], P('inst', 'tp')
The draws below stay inside these ranges and needn't reach their ends.
Inputs may be any that keep to these rules, and one draw needn't show every extreme that they name: `page_table`: the rows of one instance name each of its 128 pages exactly once. `lengths`: some request has exactly 254. `dest_instance`: the 32 requests of one instance go to 32 different instances, and every instance receives exactly 32 requests. `dest_slot`: the requests that reach one instance take its slots once each.
All inputs are finite; a program needn't handle non-finite values.
Results may differ from the reference program's by a relative error of at most 0.022.
Values may be sent and summed in bfloat16 or wider, within the bound.
A program may use at most 64 MiB of HBM per device.

```python
import jax
import jax.numpy as jnp

HD = 128
QPK = 8
DW = 4096
PAGE = 64
SLOTS = 32
PR = 4
KVH = 8
QH = 64
INSTANCES = 32
REQUESTS = 1024
POOL = 128
LMAX = 254


def plan_tables(key):
    key = jax.random.fold_in(key, 7)
    rho = jax.random.permutation(jax.random.fold_in(key, 1), INSTANCES)
    tau = jax.random.permutation(jax.random.fold_in(key, 2), INSTANCES)
    offsets = jax.random.permutation(jax.random.fold_in(key, 3), INSTANCES)[:SLOTS]
    dest = rho[(tau[:, None] + offsets[None, :]) % INSTANCES]
    keys = jax.random.split(jax.random.fold_in(key, 4), INSTANCES)
    orders = jax.vmap(lambda one: jax.random.permutation(one, SLOTS))(keys)
    columns = jnp.arange(SLOTS, dtype=jnp.int32)[None, :]
    slot = orders[dest, columns]
    return (dest.reshape(-1).astype(jnp.int32), slot.reshape(-1).astype(jnp.int32))


def draw_queries(key, salt):
    key = jax.random.fold_in(key, salt)
    shape = (REQUESTS, QH, HD)
    base = jnp.clip(jax.random.normal(key, shape, jnp.float32), -6.0, 6.0)
    return base.astype(jnp.bfloat16)


def draw_query_one(key, part):
    return draw_queries(key, 21)


def draw_query_two(key, part):
    return draw_queries(key, 22)


def draw_key_pages(key, part):
    key = jax.random.fold_in(key, 11)
    shape = (INSTANCES * POOL, KVH, PAGE, HD)
    base = jnp.clip(jax.random.normal(key, shape, jnp.float32), -6.0, 6.0)
    return base.astype(jnp.bfloat16)


def draw_page_table(key, part):
    key = jax.random.fold_in(key, 5)
    keys = jax.random.split(key, INSTANCES)
    table = jax.vmap(lambda one: jax.random.permutation(one, POOL))(keys)
    return table.reshape(REQUESTS, PR).astype(jnp.int32)


def draw_lengths(key, part):
    key = jax.random.fold_in(key, 3)
    heat = jax.random.randint(jax.random.fold_in(key, 1), (INSTANCES, 1), LMAX // 8, LMAX - 7)
    spread = jax.random.randint(jax.random.fold_in(key, 2), (INSTANCES, SLOTS), 0, 1 << 20)
    values = (8 + spread % heat).reshape(-1)
    where_most = jax.random.randint(jax.random.fold_in(key, 4), (), 0, REQUESTS)
    return values.at[where_most].set(LMAX).astype(jnp.int32)


def draw_dest_instance(key, part):
    return plan_tables(key)[0]


def draw_dest_slot(key, part):
    return plan_tables(key)[1]


def level_of(own_key, shape, shards, least, high):
    factor_of = 1.0
    for axis_at, parts in shards:
        steps = jax.random.uniform(jax.random.fold_in(jax.random.fold_in(own_key, 6), axis_at), (parts,), jnp.float32, least / len(shards), high / len(shards))
        factor_of = factor_of * jnp.repeat(jnp.exp(steps), shape[axis_at] // parts).reshape((-1,) + (1,) * (len(shape) - 1 - axis_at))
    return factor_of


def noise(rng, dims, width, reach, pieces=(), kind=jnp.bfloat16):
    drawn = width * jax.random.normal(rng, dims, jnp.float32)
    if pieces:
        drawn = drawn * level_of(rng, dims, pieces, -0.22, 0.18)
    return jnp.clip(drawn, -reach, reach).astype(kind)


def setup_inputs(seed: int = 0) -> dict:
    key_of = jax.random.split(jax.random.key(seed), 14)
    query_one = draw_query_one(jax.random.fold_in(key_of[13], 71), 0)
    key_one = noise(key_of[1], (REQUESTS, KVH, HD), 1.0, 6.0, ((0, 32), (1, 8)))
    value_one = noise(key_of[2], (REQUESTS, KVH, HD), 1.0, 6.0, ((0, 32), (1, 8)))
    key_pages = draw_key_pages(jax.random.fold_in(key_of[13], 71), 0)
    value_pages = noise(key_of[4], (INSTANCES * POOL, KVH, PAGE, HD), 1.0, 6.0, ((0, 32), (1, 8)))
    page_table = draw_page_table(jax.random.fold_in(key_of[13], 71), 0)
    lengths = draw_lengths(jax.random.fold_in(key_of[13], 71), 0)
    dest_instance = draw_dest_instance(jax.random.fold_in(key_of[13], 71), 0)
    dest_slot = draw_dest_slot(jax.random.fold_in(key_of[13], 71), 0)
    query_two = draw_query_two(jax.random.fold_in(key_of[13], 71), 0)
    key_two = noise(key_of[10], (REQUESTS, KVH, HD), 1.0, 6.0, ((0, 32), (1, 8)))
    value_two = noise(key_of[11], (REQUESTS, KVH, HD), 1.0, 6.0, ((0, 32), (1, 8)))
    out_weight = noise(key_of[12], (QH * HD, DW), (QPK * HD) ** -0.5, 0.1875, ((0, 8),))
    return {"query_one": query_one, "key_one": key_one, "value_one": value_one, "key_pages": key_pages, "value_pages": value_pages, "page_table": page_table, "lengths": lengths, "dest_instance": dest_instance, "dest_slot": dest_slot, "query_two": query_two, "key_two": key_two, "value_two": value_two, "out_weight": out_weight}


NEG = -1e30


def put_token(pages, token, position):
    rows = jnp.arange(pages.shape[0], dtype=jnp.int32)
    size = pages.shape[3]
    return pages.at[rows, position // size, :, position % size, :].set(token)


def attend(query, pages_k, pages_v, count):
    rows = query.shape[0]
    grouped = query.astype(jnp.float32).reshape(rows, KVH, QPK, HD)
    scores = jnp.einsum("rkgd,rpktd->rkgpt", grouped, pages_k.astype(jnp.float32))
    scores = scores.reshape(rows, KVH, QPK, PR * PAGE) * (HD ** -0.5)
    live = jnp.arange(PR * PAGE, dtype=jnp.int32)[None, :] < count[:, None]
    live = live[:, None, None, :]
    scores = jnp.where(live, scores, NEG)
    top = jnp.max(scores, axis=-1, keepdims=True)
    expo = jnp.where(live, jnp.exp(scores - top), 0.0)
    weights = (expo / jnp.sum(expo, axis=-1, keepdims=True)).astype(jnp.bfloat16)
    weights = weights.astype(jnp.float32).reshape(rows, KVH, QPK, PR, PAGE)
    mixed = jnp.einsum("rkgpt,rpktd->rkgd", weights, pages_v.astype(jnp.float32))
    return mixed.astype(jnp.bfloat16).reshape(rows, QH * HD)


def reference(query_one, key_one, value_one, key_pages, value_pages, page_table, lengths, dest_instance, dest_slot, query_two, key_two, value_two, out_weight):
    rows = jnp.arange(REQUESTS, dtype=jnp.int32)
    home = rows // SLOTS
    global_pages = (home[:, None] * POOL + page_table).astype(jnp.int32)
    written_k = put_token(key_pages[global_pages], key_one, lengths)
    written_v = put_token(value_pages[global_pages], value_one, lengths)
    first = attend(query_one, written_k, written_v, lengths + 1)
    out_one = jnp.dot(first, out_weight, preferred_element_type=jnp.float32).astype(jnp.bfloat16)
    target = (dest_instance * SLOTS + dest_slot).astype(jnp.int32)
    moved_k = jnp.zeros_like(written_k).at[target].set(written_k)
    moved_v = jnp.zeros_like(written_v).at[target].set(written_v)
    moved_lengths = jnp.zeros_like(lengths).at[target].set(lengths)
    moved_k = put_token(moved_k, key_two, moved_lengths + 1)
    moved_v = put_token(moved_v, value_two, moved_lengths + 1)
    second = attend(query_two, moved_k, moved_v, moved_lengths + 2)
    out_two = jnp.dot(second, out_weight, preferred_element_type=jnp.float32).astype(jnp.bfloat16)
    key_cache = moved_k.reshape(REQUESTS * PR, KVH, PAGE, HD)
    value_cache = moved_v.reshape(REQUESTS * PR, KVH, PAGE, HD)
    return (out_one, out_two, key_cache, value_cache)
```

```python
import jax
import jax.numpy as jnp
from jax import lax
from jax.experimental import pallas as pl
from jax.experimental.pallas import tpu as pltpu
from jax.sharding import PartitionSpec as P

MESH = pl.DeviceIdType.MESH
NEG = -1e30
N = 32
TP = 8
ZH = 4
PR = 4
PAGE = 64
SPAN = PR * PAGE
HD = 128
G = 8
CH = 512
WINDOW = 8
BATCH = 4
F32 = jnp.float32
BF16 = jnp.bfloat16


def iota(shape, dim):
    return lax.broadcasted_iota(jnp.int32, shape, dim)


def attend(queries, keys, values, counts):
    scores = [
        lax.dot_general(q, k, (((1,), (1,)), ((), ())), preferred_element_type=F32)
        for q, k in zip(queries, keys)
    ]
    live = jnp.concatenate([iota((G, SPAN), 1) < n for n in counts], axis=0)
    scores = jnp.concatenate(scores, axis=0) * HD ** (-0.5)
    scores = jnp.where(live, scores, NEG)
    top = jnp.max(scores, axis=-1, keepdims=True)
    expo = jnp.where(live, jnp.exp(scores - top), 0.0)
    weights = (expo / jnp.sum(expo, axis=-1, keepdims=True)).astype(BF16)
    return [
        jnp.dot(weights[i * G : (i + 1) * G], v, preferred_element_type=F32)
        for i, v in enumerate(values)
    ]


def put_token(page, token, first_row, position):
    return jnp.where(iota(page.shape, 0) + first_row == position, token, page)


def exchange_kernel(
    pt, dest_s, len_s, dest_v, slot_v, len_v, q1, k1, v1, q2, k2, v2, kp, vp, w_hbm,
    moved, hdr_r, out1, out2,
    kpv, vpv, w, send, tab_v, tab_s, hdr_s, hdr_rs, rep_s, rep_r, o1, os, orr, lhs,
    own, pa_s, pa_r, pb_s, pb_r,
    lsem, hs, hr, rs, rr, ss, sr, bs, br, psem,
):
    me, tp = lax.axis_index("inst"), lax.axis_index("tp")
    x, y, zl = me % 4, (me // 4) % 4, me // 16
    core, zh = tp % 2, tp // 2

    def load(src, dst, i):
        return pltpu.make_async_copy(src, dst, lsem.at[i])

    load(kp, kpv, 0).start()
    load(vp, vpv, 1).start()
    load(w_hbm, w, 2).start()

    barrier = pltpu.get_barrier_semaphore()

    def greet_inst(i, c):
        pl.semaphore_signal(barrier, inc=1, device_id={"inst": (me + i) % N}, device_id_type=MESH)
        return c

    def greet_tp(i, c):
        pl.semaphore_signal(barrier, inc=1, device_id={"tp": (tp + i) % TP}, device_id_type=MESH)
        return c

    lax.fori_loop(1, N, greet_inst, 0)
    lax.fori_loop(1, TP, greet_tp, 0)

    here = dest_v[...] == iota((N, N), 0)
    row = jnp.max(jnp.where(here, iota((N, N), 1), 0), axis=1, keepdims=True)
    length = jnp.max(jnp.where(here, len_v[...], 0), axis=1, keepdims=True)
    slot = jnp.max(jnp.where(here, slot_v[...], 0), axis=1, keepdims=True)
    lane = iota((N, 128), 1)
    tab_v[...] = jnp.where(lane < 32, row, jnp.where(lane < 64, length, slot))
    to_scalar = load(tab_v, tab_s, 3)
    to_scalar.start()
    to_scalar.wait()

    def header(t, c):
        hdr_s[t] = jnp.where(iota((1, 128), 1) < 64, tab_s[t, 64], tab_s[t, 32])
        return c

    lax.fori_loop(0, N, header, 0)

    def remote(src, dst, send_sem, recv_sem, device):
        return pltpu.make_async_remote_copy(
            src_ref=src, dst_ref=dst, send_sem=send_sem, recv_sem=recv_sem,
            device_id=device, device_id_type=MESH,
        )

    def each_other(body):
        def step(i, c):
            body((me + i) % N)
            return c

        lax.fori_loop(1, N, step, 0)

    def send_header(t):
        return remote(hdr_s.at[t], hdr_r.at[me], hs.at[t], hr.at[me], {"inst": t})

    def wait_header(t):
        return remote(hdr_s.at[t], hdr_r.at[t], hs.at[t], hr.at[t], {"inst": t})

    pl.semaphore_wait(barrier, N + TP - 2)
    each_other(lambda t: send_header(t).start())
    hdr_r[me] = hdr_s[me]

    def offset(k):
        i, j = k % 4, k // 4
        dx, dy, dz = i, (i + j) % 4, (i // 2 + j // 4) % 2
        return dx, dy, dz

    def target(k, sign):
        dx, dy, dz = offset(k)
        turn = sign * (1 - 2 * core)
        return (((zl + dz) % 2) * 4 + (y + 4 + turn * dy) % 4) * 4 + (x + 4 + turn * dx) % 4

    def gather(t):
        r, n = tab_s[t, 0], tab_s[t, 32]
        for which, (pages, token) in enumerate(((kpv, k1), (vpv, v1))):
            for p in range(PR):
                page = put_token(pages[pt[r, p]], token[r], p * PAGE, n)
                send[t, which, p * PAGE : (p + 1) * PAGE] = page

    def block_out(k):
        t = target(k, 1)
        return remote(send.at[t], moved.at[me], bs.at[t], br.at[me], {"inst": t})

    def block_in(k):
        s = target(k, -1)
        return remote(send.at[s], moved.at[s], bs.at[s], br.at[s], {"inst": s}), s

    load(kp, kpv, 0).wait()
    load(vp, vpv, 1).wait()

    def first_blocks(k, c):
        gather(target(k, 1))
        block_out(k).start()
        return c

    def later_blocks(k, c):
        gather(target(k, 1))
        return c

    lax.fori_loop(1, 1 + WINDOW, first_blocks, 0)
    lax.fori_loop(1 + WINDOW, N, later_blocks, 0)
    gather(me)

    def pump(k):
        block_out(k - WINDOW).wait_send()
        block_out(k).start()

    def pumps(lo, hi):
        def step(k, c):
            pump(k)
            return c

        lax.fori_loop(lo, hi, step, 0)

    def attend_one(g, c):
        rows = [g * BATCH + i for i in range(BATCH)]
        at = [dest_s[r] for r in rows]
        res = attend(
            [q1[r] for r in rows], [send[t, 0] for t in at], [send[t, 1] for t in at],
            [len_s[r] + 1 for r in rows],
        )
        for r, one in zip(rows, res):
            o1[pl.ds(pl.multiple_of(r * G, G), G), :] = one
        return c

    lax.fori_loop(0, 4, attend_one, 0)
    pumps(9, 11)

    each_other(lambda t: wait_header(t).wait())
    fetch = load(hdr_r, hdr_rs, 4)
    fetch.start()
    fetch.wait()

    def reply(s, c):
        j = hdr_rs[s, 0, 0]
        token = jnp.where(iota((G, HD), 0) == 0, k2[j].astype(F32), v2[j].astype(F32))
        rep_s[s] = jnp.concatenate([q2[j].astype(F32), token], axis=0).astype(BF16)
        return c

    lax.fori_loop(0, N, reply, 0)
    each_other(lambda s: remote(rep_s.at[s], rep_r.at[me], rs.at[s], rr.at[me], {"inst": s}).start())
    rep_r[me] = rep_s[me]
    pumps(11, 13)
    lax.fori_loop(4, 8, attend_one, 0)
    pumps(13, 15)

    def project(side, chunk):
        at = pl.multiple_of(side * (ZH * CH) + chunk * CH, CH)
        return jnp.dot(lhs[...], w[:, pl.ds(at, CH)], preferred_element_type=F32)

    def heads_side_by_side(ref):
        parts = [ref[pl.ds(h, N, stride=G), :] for h in range(G)]
        return jnp.concatenate(parts, axis=1).astype(BF16)

    other = {"tp": zh * 2 + 1 - core}

    def sum_a(i):
        def away(h, c):
            pa_s[i, h] = project(1 - core, h).astype(BF16)
            return c

        lax.fori_loop(0, ZH, away, 0)
        remote(pa_s.at[i], pa_r.at[i], psem.at[i, 0], psem.at[i, 1], other).start()

        def keep(h, c):
            own[i, h] = project(core, h)
            return c

        lax.fori_loop(0, ZH, keep, 0)

    def part_b(i, d):
        h = (zh + d) % ZH
        return remote(pb_s.at[i, h], pb_r.at[i, zh], psem.at[i, 2 + d], psem.at[i, 6 + zh], {"tp": h * 2 + core}), h

    def sum_b(i):
        remote(pa_s.at[i], pa_r.at[i], psem.at[i, 0], psem.at[i, 1], other).wait()
        for h in range(ZH):
            both = own[i, h] + pa_r[i, h].astype(F32)
            own[i, h] = both
            pb_s[i, h] = both.astype(BF16)
        for d in range(1, ZH):
            part_b(i, d)[0].start()

    outs = (out1, out2)

    def chunk_to(i, h, device, send_at, recv_at):
        at = core * ZH + h
        return remote(outs[i].at[at], outs[i].at[at], psem.at[i, send_at], psem.at[i, recv_at], device)

    def sum_c(i):
        total = own[i, zh]
        for d in range(1, ZH):
            part, h = part_b(i, d)
            part.wait_send()
            remote(pb_s.at[i, h], pb_r.at[i, h], psem.at[i, 2 + d], psem.at[i, 6 + h], {"tp": h * 2 + core}).wait_recv()
            total = total + pb_r[i, h].astype(F32)
        outs[i][core * ZH + zh] = total.astype(BF16)
        for d in range(1, ZH):
            chunk_to(i, zh, {"tp": ((zh + d) % ZH) * 2 + core}, 10 + d, 14 + zh).start()
        chunk_to(i, zh, other, 18 + zh, 22 + zh).start()

    def sum_d(i):
        for d in range(1, ZH):
            h = (zh + d) % ZH
            chunk_to(i, h, {"tp": h * 2 + core}, 10 + d, 14 + h).wait()
            chunk_to(i, h, other, 18 + h, 22 + h).start()

    def sum_end(i):
        for h in range(ZH):
            at = (1 - core) * ZH + h
            chunk_to(i, h, other, 18 + h, 22 + h).wait_send()
            remote(outs[i].at[at], outs[i].at[at], psem.at[i, 18 + h], psem.at[i, 22 + h], other).wait_recv()

    load(w_hbm, w, 2).wait()
    lhs[...] = heads_side_by_side(o1)
    sum_a(0)
    pumps(15, 17)

    each_other(lambda t: remote(rep_s.at[t], rep_r.at[t], rs.at[t], rr.at[t], {"inst": t}).wait())

    def attend_two(g):
        ts = [g * BATCH + i for i in range(BATCH)]
        tiles = [rep_r[t].astype(F32) for t in ts]
        at = [tab_s[t, 32] + 1 for t in ts]
        keys = [put_token(send[t, 0], m[G : G + 1].astype(BF16), 0, n) for t, m, n in zip(ts, tiles, at)]
        values = [put_token(send[t, 1], m[G + 1 : G + 2].astype(BF16), 0, n) for t, m, n in zip(ts, tiles, at)]
        res = attend([m[:G].astype(BF16) for m in tiles], keys, values, [n + 1 for n in at])
        for t, one in zip(ts, res):
            os[pl.ds(pl.multiple_of(t * G, G), G), :] = one.astype(BF16).astype(F32)

    def rows_of(ref, s):
        return ref.at[pl.ds(pl.multiple_of(s * G, G), G), :]

    def result_out(t):
        return remote(rows_of(os, t), rows_of(orr, me), ss.at[t], sr.at[me], {"inst": t})

    def result_in(s):
        return remote(rows_of(os, s), rows_of(orr, s), ss.at[s], sr.at[s], {"inst": s})

    def half_two(lo, hi):
        def step(g, c):
            attend_two(g)
            for i in range(BATCH):
                t = g * BATCH + i

                @pl.when(t != me)
                def _():
                    result_out(t).start()

            return c

        lax.fori_loop(lo, hi, step, 0)

    half_two(0, 4)
    sum_b(0)
    pumps(17, 20)
    half_two(4, 8)
    orr[pl.ds(pl.multiple_of(me * G, G), G), :] = os[pl.ds(pl.multiple_of(me * G, G), G), :]
    pumps(20, 22)
    sum_c(0)

    each_other(lambda s: result_in(s).wait())

    def slot_row(s, acc):
        return jnp.where(iota((1, 128), 1) == s, hdr_rs[s, 0, 0], acc)

    slots = lax.fori_loop(0, N, slot_row, jnp.zeros((1, 128), jnp.int32))
    pick = jnp.where(slots[:, :N] == iota((N, N), 0), 1.0, 0.0).astype(BF16)
    lhs[...] = jnp.dot(pick, heads_side_by_side(orr), preferred_element_type=F32).astype(BF16)
    sum_a(1)
    sum_d(0)
    pumps(22, 24)
    sum_b(1)
    pumps(24, 28)
    sum_c(1)
    sum_end(0)
    pumps(28, 32)
    sum_d(1)

    def finish(s):
        n, j = hdr_rs[s, 0, 64] + 1, hdr_rs[s, 0, 0]
        for which, token in enumerate((k2, v2)):
            moved[s, which] = put_token(moved[s, which], token[j], 0, n)

    for which in range(2):
        moved[me, which] = send[me, which]
    finish(me)

    def arrive(k, c):
        copy, s = block_in(k)
        copy.wait_recv()
        finish(s)
        return c

    lax.fori_loop(1, N, arrive, 0)

    def sent(k, c):
        block_out(k).wait_send()
        return c

    lax.fori_loop(N - WINDOW, N, sent, 0)
    sum_end(1)


def place_kernel(hdr, moved, part1, part2, out1, out2, key_cache, value_cache, sems):
    caches = (key_cache, value_cache)

    def put(s, c):
        for which, cache in enumerate(caches):
            pltpu.make_async_copy(moved.at[s, which], cache.at[hdr[s, 0, 0]], sems.at[which]).start()
        return c

    lax.fori_loop(0, N, put, 0)
    for part, out in ((part1, out1), (part2, out2)):
        for c in range(TP):
            out[:, c * CH : (c + 1) * CH] = part[c]
    for which, cache in enumerate(caches):
        pltpu.make_async_copy(moved.at[:, which], cache, sems.at[which]).wait()


def shards(
    query_one, key_one, value_one, key_pages, value_pages, page_table, lengths,
    dest_instance, dest_slot, query_two, key_two, value_two, out_weight,
):
    vmem = pl.BlockSpec(memory_space=pltpu.VMEM)
    smem = pl.BlockSpec(memory_space=pltpu.SMEM)
    hbm = pl.BlockSpec(memory_space=pl.ANY)
    columns = out_weight.shape[1]
    pool = key_pages.shape[0]
    dma = pltpu.SemaphoreType.DMA
    moved, hdr, part1, part2 = pl.pallas_call(
        exchange_kernel,
        out_shape=(
            jax.ShapeDtypeStruct((N, 2, SPAN, HD), BF16),
            jax.ShapeDtypeStruct((N, 1, 128), jnp.int32),
            jax.ShapeDtypeStruct((TP, N, CH), BF16),
            jax.ShapeDtypeStruct((TP, N, CH), BF16),
        ),
        in_specs=[smem] * 3 + [vmem] * 9 + [hbm] * 3,
        out_specs=(vmem, vmem, vmem, vmem),
        scratch_shapes=[
            pltpu.VMEM((pool, PAGE, HD), BF16),
            pltpu.VMEM((pool, PAGE, HD), BF16),
            pltpu.VMEM((G * HD, columns), BF16),
            pltpu.VMEM((N, 2, SPAN, HD), BF16),
            pltpu.VMEM((N, 128), jnp.int32),
            pltpu.SMEM((N, 128), jnp.int32),
            pltpu.VMEM((N, 1, 128), jnp.int32),
            pltpu.SMEM((N, 1, 128), jnp.int32),
            pltpu.VMEM((N, 2 * G, HD), BF16),
            pltpu.VMEM((N, 2 * G, HD), BF16),
            pltpu.VMEM((N * G, HD), F32),
            pltpu.VMEM((N * G, HD), F32),
            pltpu.VMEM((N * G, HD), F32),
            pltpu.VMEM((N, G * HD), BF16),
            pltpu.VMEM((2, ZH, N, CH), F32),
            pltpu.VMEM((2, ZH, N, CH), BF16),
            pltpu.VMEM((2, ZH, N, CH), BF16),
            pltpu.VMEM((2, ZH, N, CH), BF16),
            pltpu.VMEM((2, ZH, N, CH), BF16),
            dma((5,)),
            dma((N,)), dma((N,)), dma((N,)), dma((N,)), dma((N,)), dma((N,)), dma((N,)), dma((N,)),
            dma((2, 26)),
        ],
        compiler_params=pltpu.CompilerParams(
            collective_id=0, has_side_effects=True, vmem_limit_bytes=48 << 20
        ),
        name="exchange",
    )(
        page_table, dest_instance, lengths,
        dest_instance.reshape(1, N), dest_slot.reshape(1, N), lengths.reshape(1, N),
        query_one, key_one, value_one, query_two, key_two, value_two,
        key_pages.reshape(pool, PAGE, HD), value_pages.reshape(pool, PAGE, HD), out_weight,
    )
    out1, out2, key_cache, value_cache = pl.pallas_call(
        place_kernel,
        out_shape=(
            jax.ShapeDtypeStruct((N, columns), BF16),
            jax.ShapeDtypeStruct((N, columns), BF16),
            jax.ShapeDtypeStruct((N, SPAN, HD), BF16),
            jax.ShapeDtypeStruct((N, SPAN, HD), BF16),
        ),
        in_specs=[smem, hbm, vmem, vmem],
        out_specs=(vmem, vmem, hbm, hbm),
        scratch_shapes=[dma((2,))],
        compiler_params=pltpu.CompilerParams(vmem_limit_bytes=48 << 20),
        name="place",
    )(hdr, moved, part1, part2)
    shape = (N * PR, 1, PAGE, HD)
    return out1, out2, key_cache.reshape(shape), value_cache.reshape(shape)


def solution(mesh):
    return jax.shard_map(
        shards,
        mesh=mesh,
        in_specs=(
            P("inst", "tp", None),
            P("inst", "tp", None),
            P("inst", "tp", None),
            P("inst", "tp", None, None),
            P("inst", "tp", None, None),
            P("inst", None),
            P("inst"),
            P("inst"),
            P("inst"),
            P("inst", "tp", None),
            P("inst", "tp", None),
            P("inst", "tp", None),
            P("tp", None),
        ),
        out_specs=(
            P("inst", None),
            P("inst", None),
            P("inst", "tp", None, None),
            P("inst", "tp", None, None),
        ),
        check_vma=False,
    )
```

```python
import jax
import jax.numpy as jnp
from jax import lax
from jax.experimental import pallas as pl
from jax.experimental.pallas import tpu as pltpu
from jax.sharding import PartitionSpec as P

MESH = pl.DeviceIdType.MESH
NEG = -1e30
N = 32
TP = 8
ZH = 4
PR = 4
PAGE = 64
SPAN = PR * PAGE
HD = 128
G = 8
CH = 512
WINDOW = 8
BATCH = 4
F32 = jnp.float32
BF16 = jnp.bfloat16


def iota(shape, dim):
    return lax.broadcasted_iota(jnp.int32, shape, dim)


def attend(queries, keys, values, counts):
    scores = [
        lax.dot_general(q, k, (((1,), (1,)), ((), ())), preferred_element_type=F32)
        for q, k in zip(queries, keys)
    ]
    live = jnp.concatenate([iota((G, SPAN), 1) < n for n in counts], axis=0)
    scores = jnp.concatenate(scores, axis=0) * HD ** (-0.5)
    scores = jnp.where(live, scores, NEG)
    top = jnp.max(scores, axis=-1, keepdims=True)
    expo = jnp.where(live, jnp.exp(scores - top), 0.0)
    weights = (expo / jnp.sum(expo, axis=-1, keepdims=True)).astype(BF16)
    return [
        jnp.dot(weights[i * G : (i + 1) * G], v, preferred_element_type=F32)
        for i, v in enumerate(values)
    ]


def put_token(page, token, first_row, position):
    return jnp.where(iota(page.shape, 0) + first_row == position, token, page)


def exchange_kernel(
    pt_hbm, dest_hbm, slot_hbm, len_hbm, q1_hbm, k1_hbm, v1_hbm, q2_hbm, k2_hbm, v2_hbm, kp, vp, w_hbm,
    moved, hdr_r, out1, out2,
    pt, dest_s, len_s, dest_v, slot_v, len_v, q1, q2, tok_b, tok, kpv, vpv, w, send, tab_v, tab_s, hdr_s, hdr_rs, rep_s, rep_r, o1, os, orr, lhs,
    own, pa_s, pa_r, pb_s, pb_r,
    lsem, hs, hr, rs, rr, ss, sr, bs, br, psem,
):
    me, tp = lax.axis_index("inst"), lax.axis_index("tp")
    x, y, zl = me % 4, (me // 4) % 4, me // 16
    core, zh = tp % 2, tp // 2

    def load(src, dst, i):
        return pltpu.make_async_copy(src, dst, lsem.at[i])

    small = [
        load(src, dst, 5 + i)
        for i, (src, dst) in enumerate((
            (dest_hbm, dest_v), (slot_hbm, slot_v), (len_hbm, len_v), (pt_hbm, pt),
            (dest_hbm, dest_s), (len_hbm, len_s),
            (k1_hbm, tok_b.at[0]), (v1_hbm, tok_b.at[1]), (k2_hbm, tok_b.at[2]), (v2_hbm, tok_b.at[3]),
            (q1_hbm, q1), (q2_hbm, q2),
        ))
    ]
    for copy in small[:8]:
        copy.start()
    load(kp, kpv, 0).start()
    load(vp, vpv, 1).start()
    for copy in small[8:]:
        copy.start()
    load(w_hbm, w, 2).start()

    barrier = pltpu.get_barrier_semaphore()

    def greet_inst(i, c):
        pl.semaphore_signal(barrier, inc=1, device_id={"inst": (me + i) % N}, device_id_type=MESH)
        return c

    def greet_tp(i, c):
        pl.semaphore_signal(barrier, inc=1, device_id={"tp": (tp + i) % TP}, device_id_type=MESH)
        return c

    lax.fori_loop(1, N, greet_inst, 0)
    lax.fori_loop(1, TP, greet_tp, 0)

    for copy in small[:8]:
        copy.wait()

    here = dest_v[...] == iota((N, N), 0)
    row = jnp.max(jnp.where(here, iota((N, N), 1), 0), axis=1, keepdims=True)
    length = jnp.max(jnp.where(here, len_v[...], 0), axis=1, keepdims=True)
    slot = jnp.max(jnp.where(here, slot_v[...], 0), axis=1, keepdims=True)
    lane = iota((N, 128), 1)
    tab_v[...] = jnp.where(lane < 32, row, jnp.where(lane < 64, length, slot))
    to_scalar = load(tab_v, tab_s, 3)
    to_scalar.start()
    to_scalar.wait()

    def header(t, c):
        hdr_s[t] = jnp.where(iota((1, 128), 1) < 64, tab_s[t, 64], tab_s[t, 32])
        return c

    lax.fori_loop(0, N, header, 0)

    def remote(src, dst, send_sem, recv_sem, device):
        return pltpu.make_async_remote_copy(
            src_ref=src, dst_ref=dst, send_sem=send_sem, recv_sem=recv_sem,
            device_id=device, device_id_type=MESH,
        )

    def each_other(body):
        def step(i, c):
            body((me + i) % N)
            return c

        lax.fori_loop(1, N, step, 0)

    def send_header(t):
        return remote(hdr_s.at[t], hdr_r.at[me], hs.at[t], hr.at[me], {"inst": t})

    def wait_header(t):
        return remote(hdr_s.at[t], hdr_r.at[t], hs.at[t], hr.at[t], {"inst": t})

    pl.semaphore_wait(barrier, N + TP - 2)
    each_other(lambda t: send_header(t).start())
    hdr_r[me] = hdr_s[me]

    def offset(k):
        i, j = k % 4, k // 4
        dx, dy, dz = i, (i + j) % 4, (i // 2 + j // 4) % 2
        return dx, dy, dz

    def target(k, sign):
        dx, dy, dz = offset(k)
        turn = sign * (1 - 2 * core)
        return (((zl + dz) % 2) * 4 + (y + 4 + turn * dy) % 4) * 4 + (x + 4 + turn * dx) % 4

    def gather(t):
        r, n = tab_s[t, 0], tab_s[t, 32]
        for which, pages in enumerate((kpv, vpv)):
            token = tok[which, pl.ds(r, 1), :].astype(BF16)
            for p in range(PR):
                page = put_token(pages[pt[p, r]], token, p * PAGE, n)
                send[t, which, p * PAGE : (p + 1) * PAGE] = page

    def block_out(k):
        t = target(k, 1)
        return remote(send.at[t], moved.at[me], bs.at[t], br.at[me], {"inst": t})

    def block_in(k):
        s = target(k, -1)
        return remote(send.at[s], moved.at[s], bs.at[s], br.at[s], {"inst": s}), s

    for copy in small[8:]:
        copy.wait()
    tok[...] = tok_b[...].astype(F32)
    load(kp, kpv, 0).wait()
    load(vp, vpv, 1).wait()

    def first_blocks(k, c):
        gather(target(k, 1))
        block_out(k).start()
        return c

    def later_blocks(k, c):
        gather(target(k, 1))
        return c

    lax.fori_loop(1, 1 + WINDOW, first_blocks, 0)
    lax.fori_loop(1 + WINDOW, N, later_blocks, 0)
    gather(me)

    def pump(k):
        block_out(k - WINDOW).wait_send()
        block_out(k).start()

    def pumps(lo, hi):
        def step(k, c):
            pump(k)
            return c

        lax.fori_loop(lo, hi, step, 0)

    def attend_one(g, c):
        rows = [g * BATCH + i for i in range(BATCH)]
        at = [dest_s[0, r] for r in rows]
        res = attend(
            [q1[r] for r in rows], [send[t, 0] for t in at], [send[t, 1] for t in at],
            [len_s[0, r] + 1 for r in rows],
        )
        for r, one in zip(rows, res):
            o1[pl.ds(pl.multiple_of(r * G, G), G), :] = one
        return c

    lax.fori_loop(0, 4, attend_one, 0)
    pumps(9, 11)

    each_other(lambda t: wait_header(t).wait())
    fetch = load(hdr_r, hdr_rs, 4)
    fetch.start()
    fetch.wait()

    def reply(s, c):
        j = hdr_rs[s, 0, 0]
        token = jnp.where(iota((G, HD), 0) == 0, tok[2, pl.ds(j, 1), :], tok[3, pl.ds(j, 1), :])
        rep_s[s] = jnp.concatenate([q2[j].astype(F32), token], axis=0).astype(BF16)
        return c

    lax.fori_loop(0, N, reply, 0)
    each_other(lambda s: remote(rep_s.at[s], rep_r.at[me], rs.at[s], rr.at[me], {"inst": s}).start())
    rep_r[me] = rep_s[me]
    pumps(11, 13)
    lax.fori_loop(4, 8, attend_one, 0)
    pumps(13, 15)

    def project(side, chunk):
        at = pl.multiple_of(side * (ZH * CH) + chunk * CH, CH)
        return jnp.dot(lhs[...], w[:, pl.ds(at, CH)], preferred_element_type=F32)

    def heads_side_by_side(ref):
        parts = [ref[pl.ds(h, N, stride=G), :] for h in range(G)]
        return jnp.concatenate(parts, axis=1).astype(BF16)

    other = {"tp": zh * 2 + 1 - core}

    def sum_a(i):
        def away(h, c):
            pa_s[i, h] = project(1 - core, h).astype(BF16)
            return c

        lax.fori_loop(0, ZH, away, 0)
        remote(pa_s.at[i], pa_r.at[i], psem.at[i, 0], psem.at[i, 1], other).start()

        def keep(h, c):
            own[i, h] = project(core, h)
            return c

        lax.fori_loop(0, ZH, keep, 0)

    def part_b(i, d):
        h = (zh + d) % ZH
        return remote(pb_s.at[i, h], pb_r.at[i, zh], psem.at[i, 2 + d], psem.at[i, 6 + zh], {"tp": h * 2 + core}), h

    def sum_b(i):
        remote(pa_s.at[i], pa_r.at[i], psem.at[i, 0], psem.at[i, 1], other).wait()
        for h in range(ZH):
            both = own[i, h] + pa_r[i, h].astype(F32)
            own[i, h] = both
            pb_s[i, h] = both.astype(BF16)
        for d in range(1, ZH):
            part_b(i, d)[0].start()

    outs = (out1, out2)

    def chunk_to(i, h, device, send_at, recv_at):
        at = core * ZH + h
        return remote(outs[i].at[at], outs[i].at[at], psem.at[i, send_at], psem.at[i, recv_at], device)

    def sum_c(i):
        total = own[i, zh]
        for d in range(1, ZH):
            part, h = part_b(i, d)
            part.wait_send()
            remote(pb_s.at[i, h], pb_r.at[i, h], psem.at[i, 2 + d], psem.at[i, 6 + h], {"tp": h * 2 + core}).wait_recv()
            total = total + pb_r[i, h].astype(F32)
        outs[i][core * ZH + zh] = total.astype(BF16)
        for d in range(1, ZH):
            chunk_to(i, zh, {"tp": ((zh + d) % ZH) * 2 + core}, 10 + d, 14 + zh).start()
        chunk_to(i, zh, other, 18 + zh, 22 + zh).start()

    def sum_d(i):
        for d in range(1, ZH):
            h = (zh + d) % ZH
            chunk_to(i, h, {"tp": h * 2 + core}, 10 + d, 14 + h).wait()
            chunk_to(i, h, other, 18 + h, 22 + h).start()

    def sum_end(i):
        for h in range(ZH):
            at = (1 - core) * ZH + h
            chunk_to(i, h, other, 18 + h, 22 + h).wait_send()
            remote(outs[i].at[at], outs[i].at[at], psem.at[i, 18 + h], psem.at[i, 22 + h], other).wait_recv()

    load(w_hbm, w, 2).wait()
    lhs[...] = heads_side_by_side(o1)
    sum_a(0)
    pumps(15, 17)

    each_other(lambda t: remote(rep_s.at[t], rep_r.at[t], rs.at[t], rr.at[t], {"inst": t}).wait())

    def attend_two(g):
        ts = [g * BATCH + i for i in range(BATCH)]
        tiles = [rep_r[t].astype(F32) for t in ts]
        at = [tab_s[t, 32] + 1 for t in ts]
        keys = [put_token(send[t, 0], m[G : G + 1].astype(BF16), 0, n) for t, m, n in zip(ts, tiles, at)]
        values = [put_token(send[t, 1], m[G + 1 : G + 2].astype(BF16), 0, n) for t, m, n in zip(ts, tiles, at)]
        res = attend([m[:G].astype(BF16) for m in tiles], keys, values, [n + 1 for n in at])
        for t, one in zip(ts, res):
            os[pl.ds(pl.multiple_of(t * G, G), G), :] = one.astype(BF16).astype(F32)

    def rows_of(ref, s):
        return ref.at[pl.ds(pl.multiple_of(s * G, G), G), :]

    def result_out(t):
        return remote(rows_of(os, t), rows_of(orr, me), ss.at[t], sr.at[me], {"inst": t})

    def result_in(s):
        return remote(rows_of(os, s), rows_of(orr, s), ss.at[s], sr.at[s], {"inst": s})

    def half_two(lo, hi):
        def step(g, c):
            attend_two(g)
            for i in range(BATCH):
                t = g * BATCH + i

                @pl.when(t != me)
                def _():
                    result_out(t).start()

            return c

        lax.fori_loop(lo, hi, step, 0)

    half_two(0, 4)
    sum_b(0)
    pumps(17, 20)
    half_two(4, 8)
    orr[pl.ds(pl.multiple_of(me * G, G), G), :] = os[pl.ds(pl.multiple_of(me * G, G), G), :]
    pumps(20, 22)
    sum_c(0)

    each_other(lambda s: result_in(s).wait())

    def slot_row(s, acc):
        return jnp.where(iota((1, 128), 1) == s, hdr_rs[s, 0, 0], acc)

    slots = lax.fori_loop(0, N, slot_row, jnp.zeros((1, 128), jnp.int32))
    pick = jnp.where(slots[:, :N] == iota((N, N), 0), 1.0, 0.0).astype(BF16)
    lhs[...] = jnp.dot(pick, heads_side_by_side(orr), preferred_element_type=F32).astype(BF16)
    sum_a(1)
    sum_d(0)
    pumps(22, 24)
    sum_b(1)
    pumps(24, 28)
    sum_c(1)
    sum_end(0)
    pumps(28, 32)
    sum_d(1)

    def finish(s):
        n, j = hdr_rs[s, 0, 64] + 1, hdr_rs[s, 0, 0]
        for which in range(2):
            token = tok[2 + which, pl.ds(j, 1), :].astype(BF16)
            moved[s, which] = put_token(moved[s, which], token, 0, n)

    for which in range(2):
        moved[me, which] = send[me, which]
    finish(me)

    def arrive(k, c):
        copy, s = block_in(k)
        copy.wait_recv()
        finish(s)
        return c

    lax.fori_loop(1, N, arrive, 0)

    def sent(k, c):
        block_out(k).wait_send()
        return c

    lax.fori_loop(N - WINDOW, N, sent, 0)
    sum_end(1)


def place_kernel(hdr, moved, part1, part2, out1, out2, key_cache, value_cache, sems):
    caches = (key_cache, value_cache)

    def put(s, c):
        for which, cache in enumerate(caches):
            pltpu.make_async_copy(moved.at[s, which], cache.at[hdr[s, 0, 0]], sems.at[which]).start()
        return c

    lax.fori_loop(0, N, put, 0)
    for part, out in ((part1, out1), (part2, out2)):
        for c in range(TP):
            out[:, c * CH : (c + 1) * CH] = part[c]
    for which, cache in enumerate(caches):
        pltpu.make_async_copy(moved.at[:, which], cache, sems.at[which]).wait()


def shards(
    query_one, key_one, value_one, key_pages, value_pages, page_table, lengths,
    dest_instance, dest_slot, query_two, key_two, value_two, out_weight,
):
    vmem = pl.BlockSpec(memory_space=pltpu.VMEM)
    smem = pl.BlockSpec(memory_space=pltpu.SMEM)
    hbm = pl.BlockSpec(memory_space=pltpu.HBM)
    columns = out_weight.shape[1]
    pool = key_pages.shape[0]
    dma = pltpu.SemaphoreType.DMA
    moved, hdr, part1, part2 = pl.pallas_call(
        exchange_kernel,
        out_shape=(
            pltpu.VMEM((N, 2, SPAN, HD), BF16),
            pltpu.VMEM((N, 1, 128), jnp.int32),
            pltpu.VMEM((TP, N, CH), BF16),
            pltpu.VMEM((TP, N, CH), BF16),
        ),
        in_specs=[hbm] * 13,
        out_specs=(vmem, vmem, vmem, vmem),
        scratch_shapes=[
            pltpu.SMEM((PR, N), jnp.int32),
            pltpu.SMEM((1, N), jnp.int32),
            pltpu.SMEM((1, N), jnp.int32),
            pltpu.VMEM((1, N), jnp.int32),
            pltpu.VMEM((1, N), jnp.int32),
            pltpu.VMEM((1, N), jnp.int32),
            pltpu.VMEM((N, G, HD), BF16),
            pltpu.VMEM((N, G, HD), BF16),
            pltpu.VMEM((4, N, HD), BF16),
            pltpu.VMEM((4, N, HD), F32),
            pltpu.VMEM((pool, PAGE, HD), BF16),
            pltpu.VMEM((pool, PAGE, HD), BF16),
            pltpu.VMEM((G * HD, columns), BF16),
            pltpu.VMEM((N, 2, SPAN, HD), BF16),
            pltpu.VMEM((N, 128), jnp.int32),
            pltpu.SMEM((N, 128), jnp.int32),
            pltpu.VMEM((N, 1, 128), jnp.int32),
            pltpu.SMEM((N, 1, 128), jnp.int32),
            pltpu.VMEM((N, 2 * G, HD), BF16),
            pltpu.VMEM((N, 2 * G, HD), BF16),
            pltpu.VMEM((N * G, HD), F32),
            pltpu.VMEM((N * G, HD), F32),
            pltpu.VMEM((N * G, HD), F32),
            pltpu.VMEM((N, G * HD), BF16),
            pltpu.VMEM((2, ZH, N, CH), F32),
            pltpu.VMEM((2, ZH, N, CH), BF16),
            pltpu.VMEM((2, ZH, N, CH), BF16),
            pltpu.VMEM((2, ZH, N, CH), BF16),
            pltpu.VMEM((2, ZH, N, CH), BF16),
            dma((17,)),
            dma((N,)), dma((N,)), dma((N,)), dma((N,)), dma((N,)), dma((N,)), dma((N,)), dma((N,)),
            dma((2, 26)),
        ],
        compiler_params=pltpu.CompilerParams(
            collective_id=0, has_side_effects=True, vmem_limit_bytes=59 << 20
        ),
        name="exchange",
    )(
        page_table.T, dest_instance.reshape(1, N), dest_slot.reshape(1, N), lengths.reshape(1, N),
        query_one, key_one.reshape(N, HD), value_one.reshape(N, HD),
        query_two, key_two.reshape(N, HD), value_two.reshape(N, HD),
        key_pages.reshape(pool, PAGE, HD), value_pages.reshape(pool, PAGE, HD), out_weight,
    )
    out1, out2, key_cache, value_cache = pl.pallas_call(
        place_kernel,
        out_shape=(
            jax.ShapeDtypeStruct((N, columns), BF16),
            jax.ShapeDtypeStruct((N, columns), BF16),
            jax.ShapeDtypeStruct((N, SPAN, HD), BF16),
            jax.ShapeDtypeStruct((N, SPAN, HD), BF16),
        ),
        in_specs=[smem, vmem, vmem, vmem],
        out_specs=(vmem, vmem, hbm, hbm),
        scratch_shapes=[dma((2,))],
        compiler_params=pltpu.CompilerParams(vmem_limit_bytes=48 << 20),
        name="place",
    )(hdr, *(pltpu.with_memory_space_constraint(a, pltpu.VMEM) for a in (moved, part1, part2)))
    shape = (N * PR, 1, PAGE, HD)
    return out1, out2, key_cache.reshape(shape), value_cache.reshape(shape)


def solution(mesh):
    return jax.shard_map(
        shards,
        mesh=mesh,
        in_specs=(
            P("inst", "tp", None),
            P("inst", "tp", None),
            P("inst", "tp", None),
            P("inst", "tp", None, None),
            P("inst", "tp", None, None),
            P("inst", None),
            P("inst"),
            P("inst"),
            P("inst"),
            P("inst", "tp", None),
            P("inst", "tp", None),
            P("inst", "tp", None),
            P("tp", None),
        ),
        out_specs=(
            P("inst", None),
            P("inst", None),
            P("inst", "tp", None, None),
            P("inst", "tp", None, None),
        ),
        check_vma=False,
    )
```

```python
import jax
import jax.numpy as jnp
from jax import lax
from jax.experimental import pallas as pl
from jax.experimental.pallas import tpu as pltpu
from jax.sharding import PartitionSpec as P

MESH = pl.DeviceIdType.MESH
NEG = -1e30
N = 32
TP = 8
ZH = 4
PR = 4
PAGE = 64
SPAN = PR * PAGE
HD = 128
G = 8
CH = 512
QUARTERS = 4
HALF = SPAN // 2
BATCH = 8
PIECES = N * QUARTERS
WINDOW = 14
F32 = jnp.float32
BF16 = jnp.bfloat16


def iota(shape, dim):
    return lax.broadcasted_iota(jnp.int32, shape, dim)


def attend(queries, keys, values, counts):
    scores = [
        lax.dot_general(q, k, (((1,), (1,)), ((), ())), preferred_element_type=F32)
        for q, k in zip(queries, keys)
    ]
    live = jnp.concatenate([iota((G, SPAN), 1) < n for n in counts], axis=0)
    scores = jnp.concatenate(scores, axis=0) * HD ** (-0.5)
    scores = jnp.where(live, scores, NEG)
    top = jnp.max(scores, axis=-1, keepdims=True)
    expo = jnp.where(live, jnp.exp(scores - top), 0.0)
    weights = (expo / jnp.sum(expo, axis=-1, keepdims=True)).astype(BF16)
    return [
        jnp.dot(weights[i * G : (i + 1) * G], v, preferred_element_type=F32)
        for i, v in enumerate(values)
    ]


def put_token(page, token, first_row, position):
    return jnp.where(iota(page.shape, 0) + first_row == position, token, page)


def exchange_kernel(
    pt_hbm, dest_hbm, slot_hbm, len_hbm, q1_hbm, k1_hbm, v1_hbm, q2_hbm, k2_hbm, v2_hbm, kp, vp, w_hbm,
    moved, hdr_r, out1, out2,
    pt, dest_s, len_s, dest_v, slot_v, len_v, q1, q2, tok_b, tok, kpv, vpv, w, send, tab_v, tab_s, hdr_s, hdr_rs, rep_s, rep_r, o1, os, orr, lhs,
    own, pa_s, pa_r, pb_s, pb_r,
    lsem, hs, hr, rs, rr, ss, sr, bs, br, psem,
):
    me, tp = lax.axis_index("inst"), lax.axis_index("tp")
    x, y, zl = me % 4, (me // 4) % 4, me // 16
    core, zh = tp % 2, tp // 2

    def load(src, dst, i):
        return pltpu.make_async_copy(src, dst, lsem.at[i])

    small = [
        load(src, dst, 5 + i)
        for i, (src, dst) in enumerate((
            (dest_hbm, dest_v), (slot_hbm, slot_v), (len_hbm, len_v), (pt_hbm, pt),
            (dest_hbm, dest_s), (len_hbm, len_s),
            (k1_hbm, tok_b.at[0]), (v1_hbm, tok_b.at[1]), (k2_hbm, tok_b.at[2]), (v2_hbm, tok_b.at[3]),
            (q1_hbm, q1), (q2_hbm, q2),
        ))
    ]
    for copy in small[:8]:
        copy.start()
    load(kp, kpv, 0).start()
    load(vp, vpv, 1).start()
    for copy in small[8:]:
        copy.start()
    load(w_hbm, w, 2).start()

    barrier = pltpu.get_barrier_semaphore()

    def greet_inst(i, c):
        pl.semaphore_signal(barrier, inc=1, device_id={"inst": (me + i) % N}, device_id_type=MESH)
        return c

    def greet_tp(i, c):
        pl.semaphore_signal(barrier, inc=1, device_id={"tp": (tp + i) % TP}, device_id_type=MESH)
        return c

    lax.fori_loop(1, N, greet_inst, 0)
    lax.fori_loop(1, TP, greet_tp, 0)

    for copy in small[:8]:
        copy.wait()

    here = dest_v[...] == iota((N, N), 0)
    row = jnp.max(jnp.where(here, iota((N, N), 1), 0), axis=1, keepdims=True)
    length = jnp.max(jnp.where(here, len_v[...], 0), axis=1, keepdims=True)
    slot = jnp.max(jnp.where(here, slot_v[...], 0), axis=1, keepdims=True)
    lane = iota((N, 128), 1)
    tab_v[...] = jnp.where(lane < 32, row, jnp.where(lane < 64, length, slot))
    to_scalar = load(tab_v, tab_s, 3)
    to_scalar.start()
    to_scalar.wait()

    def header(t, c):
        hdr_s[t] = jnp.where(iota((1, 128), 1) < 64, tab_s[t, 64], tab_s[t, 32])
        return c

    lax.fori_loop(0, N, header, 0)

    def remote(src, dst, send_sem, recv_sem, device):
        return pltpu.make_async_remote_copy(
            src_ref=src, dst_ref=dst, send_sem=send_sem, recv_sem=recv_sem,
            device_id=device, device_id_type=MESH,
        )

    def each_other(body):
        def step(i, c):
            body((me + i) % N)
            return c

        lax.fori_loop(1, N, step, 0)

    def send_header(t):
        return remote(hdr_s.at[t], hdr_r.at[me], hs.at[t], hr.at[me], {"inst": t})

    def wait_header(t):
        return remote(hdr_s.at[t], hdr_r.at[t], hs.at[t], hr.at[t], {"inst": t})

    pl.semaphore_wait(barrier, N + TP - 2)
    each_other(lambda t: send_header(t).start())
    hdr_r[me] = hdr_s[me]

    def offset(k):
        i, j = k % 4, k // 4
        dx, dy, dz = i, (i + j) % 4, (i // 2 + j // 4) % 2
        return dx, dy, dz

    def target(k, sign):
        dx, dy, dz = offset(k)
        turn = sign * (1 - 2 * core)
        return (((zl + dz) % 2) * 4 + (y + 4 + turn * dy) % 4) * 4 + (x + 4 + turn * dx) % 4

    def gather(t):
        r, n = tab_s[t, 0], tab_s[t, 32]
        for which, pages in enumerate((kpv, vpv)):
            token = tok[which, pl.ds(r, 1), :].astype(BF16)
            for p in range(PR):
                page = put_token(pages[pt[p, r]], token, p * PAGE, n)
                at = p * PAGE % HALF
                send[t, which * 2 + p * PAGE // HALF, at : at + PAGE] = page

    def gathers(lo, hi):
        def step(k, c):
            gather(target(k, 1))
            return c

        lax.fori_loop(lo, hi, step, 0)

    def piece(v):
        k, quarter = v // (BATCH * QUARTERS) * BATCH + v % BATCH, v // BATCH % QUARTERS
        t = target(k, 1)
        return k, remote(send.at[t, quarter], moved.at[me, quarter], bs.at[v % 16], br.at[me], {"inst": t})

    def piece_start(v):
        k, copy = piece(v)

        @pl.when(k != 0)
        def _():
            copy.start()

    def piece_sent(v):
        k, copy = piece(v)

        @pl.when(k != 0)
        def _():
            copy.wait_send()

    def pumps(lo, hi):
        def step(v, c):
            piece_sent(v - WINDOW)
            piece_start(v)
            return c

        lax.fori_loop(lo, hi, step, 0)

    def cache_of(ref, t):
        return [ref[t, 2 * which : 2 * which + 2].reshape(SPAN, HD) for which in range(2)]

    def block_in(k):
        s = target(k, -1)
        return remote(send.at[s], moved.at[s], bs.at[0], br.at[s], {"inst": s}), s

    for copy in small[8:]:
        copy.wait()
    tok[...] = tok_b[...].astype(F32)
    load(kp, kpv, 0).wait()
    load(vp, vpv, 1).wait()
    gathers(0, BATCH)

    def begin(v, c):
        piece_start(v)
        return c

    lax.fori_loop(0, WINDOW, begin, 0)
    gathers(BATCH, 2 * BATCH)
    pumps(14, 16)
    gathers(2 * BATCH, N)
    pumps(16, 18)

    def attend_one(g, c):
        rows = [g * BATCH + i for i in range(BATCH)]
        caches = [cache_of(send, dest_s[0, r]) for r in rows]
        res = attend(
            [q1[r] for r in rows], [k for k, _ in caches], [v for _, v in caches],
            [len_s[0, r] + 1 for r in rows],
        )
        for r, one in zip(rows, res):
            o1[pl.ds(pl.multiple_of(r * G, G), G), :] = one
        pumps(18 + 2 * g, 20 + 2 * g)
        return c

    lax.fori_loop(0, N // BATCH, attend_one, 0)

    each_other(lambda t: wait_header(t).wait())
    fetch = load(hdr_r, hdr_rs, 4)
    fetch.start()
    fetch.wait()

    def reply(s):
        j = hdr_rs[s, 0, 0]
        token = jnp.where(iota((G, HD), 0) == 0, tok[2, pl.ds(j, 1), :], tok[3, pl.ds(j, 1), :])
        rep_s[s] = jnp.concatenate([q2[j].astype(F32), token], axis=0).astype(BF16)

    def reply_to(s):
        reply(s)
        remote(rep_s.at[s], rep_r.at[me], rs.at[s], rr.at[me], {"inst": s}).start()

    each_other(reply_to)
    reply(me)
    rep_r[me] = rep_s[me]
    pumps(26, 32)

    def project(side, chunk):
        at = pl.multiple_of(side * (ZH * CH) + chunk * CH, CH)
        return jnp.dot(lhs[...], w[:, pl.ds(at, CH)], preferred_element_type=F32)

    def heads_side_by_side(ref):
        parts = [ref[pl.ds(h, N, stride=G), :] for h in range(G)]
        return jnp.concatenate(parts, axis=1).astype(BF16)

    other = {"tp": zh * 2 + 1 - core}

    def sum_a(i, v):
        def away(h, c):
            pa_s[i, h] = project(1 - core, h).astype(BF16)
            pumps(v + h, v + h + 1)
            return c

        lax.fori_loop(0, ZH, away, 0)
        remote(pa_s.at[i], pa_r.at[i], psem.at[i, 0], psem.at[i, 1], other).start()

        def keep(h, c):
            own[i, h] = project(core, h)
            pumps(v + ZH + h, v + ZH + h + 1)
            return c

        lax.fori_loop(0, ZH, keep, 0)

    def part_b(i, d):
        h = (zh + d) % ZH
        return remote(pb_s.at[i, h], pb_r.at[i, zh], psem.at[i, 2 + d], psem.at[i, 6 + zh], {"tp": h * 2 + core}), h

    def sum_b(i):
        remote(pa_s.at[i], pa_r.at[i], psem.at[i, 0], psem.at[i, 1], other).wait()
        for h in range(ZH):
            both = own[i, h] + pa_r[i, h].astype(F32)
            own[i, h] = both
            pb_s[i, h] = both.astype(BF16)
        for d in range(1, ZH):
            part_b(i, d)[0].start()

    outs = (out1, out2)

    def chunk_to(i, h, device, send_at, recv_at):
        at = core * ZH + h
        return remote(outs[i].at[at], outs[i].at[at], psem.at[i, send_at], psem.at[i, recv_at], device)

    def sum_c(i):
        total = own[i, zh]
        for d in range(1, ZH):
            part, h = part_b(i, d)
            part.wait_send()
            remote(pb_s.at[i, h], pb_r.at[i, h], psem.at[i, 2 + d], psem.at[i, 6 + h], {"tp": h * 2 + core}).wait_recv()
            total = total + pb_r[i, h].astype(F32)
        outs[i][core * ZH + zh] = total.astype(BF16)
        for d in range(1, ZH):
            chunk_to(i, zh, {"tp": ((zh + d) % ZH) * 2 + core}, 10 + d, 14 + zh).start()
        chunk_to(i, zh, other, 18 + zh, 22 + zh).start()

    def sum_d(i):
        for d in range(1, ZH):
            h = (zh + d) % ZH
            chunk_to(i, h, {"tp": h * 2 + core}, 10 + d, 14 + h).wait()
            chunk_to(i, h, other, 18 + h, 22 + h).start()

    def sum_end(i):
        for h in range(ZH):
            at = (1 - core) * ZH + h
            chunk_to(i, h, other, 18 + h, 22 + h).wait_send()
            remote(outs[i].at[at], outs[i].at[at], psem.at[i, 18 + h], psem.at[i, 22 + h], other).wait_recv()

    load(w_hbm, w, 2).wait()
    lhs[...] = heads_side_by_side(o1)
    sum_a(0, 32)
    pumps(40, 44)
    sum_b(0)
    pumps(44, 54)

    each_other(lambda t: remote(rep_s.at[t], rep_r.at[t], rs.at[t], rr.at[t], {"inst": t}).wait())

    def result_out(t):
        return remote(os.at[t], orr.at[me], ss.at[t], sr.at[me], {"inst": t})

    def result_in(s):
        return remote(os.at[s], orr.at[s], ss.at[s], sr.at[s], {"inst": s})

    def attend_two(g, v, keep):
        ts = [target(g * BATCH + i, 1) for i in range(BATCH)]
        tiles = [rep_r[t].astype(F32) for t in ts]
        at = [tab_s[t, 32] + 1 for t in ts]
        caches = [
            [put_token(c, m[G + i : G + i + 1].astype(BF16), 0, n) for i, c in enumerate(cache_of(send, t))]
            for t, m, n in zip(ts, tiles, at)
        ]
        if keep:
            for t, cache in zip(ts, caches):
                for which, c in enumerate(cache):
                    send[t, 2 * which : 2 * which + 2] = c.reshape(2, HALF, HD)
        res = attend(
            [m[:G].astype(BF16) for m in tiles], [k for k, _ in caches], [v for _, v in caches],
            [n + 1 for n in at],
        )
        for t, one in zip(ts, res):
            os[t] = one.astype(BF16)
        for i, t in enumerate(ts):

            @pl.when(g * BATCH + i != 0)
            def _():
                result_out(t).start()

        pumps(v, v + 2)

    def late_blocks(g, c):
        attend_two(g, 54 + 2 * (g - 2), True)
        return c

    def early_blocks(g, c):
        attend_two(g, 58 + 2 * g, False)
        return c

    lax.fori_loop(2, 4, late_blocks, 0)
    lax.fori_loop(0, 2, early_blocks, 0)
    orr[me] = os[me]
    pumps(62, 70)
    sum_c(0)
    pumps(70, 80)

    each_other(lambda s: result_in(s).wait())
    o1[...] = orr[...].astype(F32).reshape(N * G, HD)

    def slot_row(s, acc):
        return jnp.where(iota((1, 128), 1) == s, hdr_rs[s, 0, 0], acc)

    slots = lax.fori_loop(0, N, slot_row, jnp.zeros((1, 128), jnp.int32))
    pick = jnp.where(slots[:, :N] == iota((N, N), 0), 1.0, 0.0).astype(BF16)
    lhs[...] = jnp.dot(pick, heads_side_by_side(o1), preferred_element_type=F32).astype(BF16)
    sum_a(1, 80)
    sum_d(0)

    def finish(s):
        n, j = hdr_rs[s, 0, 64] + 1, hdr_rs[s, 0, 0]
        for which, page in enumerate(cache_of(moved, s)):
            token = tok[2 + which, pl.ds(j, 1), :].astype(BF16)
            moved[s, 2 * which : 2 * which + 2] = put_token(page, token, 0, n).reshape(2, HALF, HD)

    def arrive(k, c):
        copy, s = block_in(k)
        copy.wait_recv()
        finish(s)
        return c

    def arrive_late(k, c):
        copy, _ = block_in(k)
        copy.wait_recv()
        return c

    moved[me] = send[me]
    finish(me)
    lax.fori_loop(1, BATCH, arrive, 0)
    pumps(88, 92)
    sum_b(1)
    pumps(92, 108)
    sum_end(0)
    sum_c(1)
    lax.fori_loop(BATCH, 2 * BATCH, arrive, 0)
    pumps(108, PIECES)
    sum_d(1)

    def sent(v, c):
        piece_sent(v)
        return c

    lax.fori_loop(PIECES - WINDOW, PIECES, sent, 0)
    lax.fori_loop(2 * BATCH, N, arrive_late, 0)
    sum_end(1)


def place_kernel(hdr, moved, part1, part2, out1, out2, key_cache, value_cache, sems):
    caches = (key_cache, value_cache)
    columns = [
        pltpu.make_async_copy(part.at[c], out.at[:, pl.ds(c * CH, CH)], sems.at[2 + i * TP + c])
        for i, (part, out) in enumerate(((part1, out1), (part2, out2)))
        for c in range(TP)
    ]

    def put(s, c):
        for which, cache in enumerate(caches):
            half = moved.at[s, pl.ds(2 * which, 2)]
            pltpu.make_async_copy(half, cache.at[hdr[s, 0, 0]], sems.at[which]).start()
        return c

    lax.fori_loop(0, N, put, 0, unroll=4)
    for copy in columns:
        copy.start()
    for copy in columns:
        copy.wait()
    for which, cache in enumerate(caches):
        pltpu.make_async_copy(moved.at[:, pl.ds(2 * which, 2)], cache, sems.at[which]).wait()


def shards(
    query_one, key_one, value_one, key_pages, value_pages, page_table, lengths,
    dest_instance, dest_slot, query_two, key_two, value_two, out_weight,
):
    vmem = pl.BlockSpec(memory_space=pltpu.VMEM)
    smem = pl.BlockSpec(memory_space=pltpu.SMEM)
    hbm = pl.BlockSpec(memory_space=pltpu.HBM)
    columns = out_weight.shape[1]
    pool = key_pages.shape[0]
    dma = pltpu.SemaphoreType.DMA
    moved, hdr, part1, part2 = pl.pallas_call(
        exchange_kernel,
        out_shape=(
            pltpu.VMEM((N, QUARTERS, HALF, HD), BF16),
            pltpu.VMEM((N, 1, 128), jnp.int32),
            pltpu.VMEM((TP, N, CH), BF16),
            pltpu.VMEM((TP, N, CH), BF16),
        ),
        in_specs=[hbm] * 13,
        out_specs=(vmem, vmem, vmem, vmem),
        scratch_shapes=[
            pltpu.SMEM((PR, N), jnp.int32),
            pltpu.SMEM((1, N), jnp.int32),
            pltpu.SMEM((1, N), jnp.int32),
            pltpu.VMEM((1, N), jnp.int32),
            pltpu.VMEM((1, N), jnp.int32),
            pltpu.VMEM((1, N), jnp.int32),
            pltpu.VMEM((N, G, HD), BF16),
            pltpu.VMEM((N, G, HD), BF16),
            pltpu.VMEM((4, N, HD), BF16),
            pltpu.VMEM((4, N, HD), F32),
            pltpu.VMEM((pool, PAGE, HD), BF16),
            pltpu.VMEM((pool, PAGE, HD), BF16),
            pltpu.VMEM((G * HD, columns), BF16),
            pltpu.VMEM((N, QUARTERS, HALF, HD), BF16),
            pltpu.VMEM((N, 128), jnp.int32),
            pltpu.SMEM((N, 128), jnp.int32),
            pltpu.VMEM((N, 1, 128), jnp.int32),
            pltpu.SMEM((N, 1, 128), jnp.int32),
            pltpu.VMEM((N, 2 * G, HD), BF16),
            pltpu.VMEM((N, 2 * G, HD), BF16),
            pltpu.VMEM((N * G, HD), F32),
            pltpu.VMEM((N, G, HD), BF16),
            pltpu.VMEM((N, G, HD), BF16),
            pltpu.VMEM((N, G * HD), BF16),
            pltpu.VMEM((2, ZH, N, CH), F32),
            pltpu.VMEM((2, ZH, N, CH), BF16),
            pltpu.VMEM((2, ZH, N, CH), BF16),
            pltpu.VMEM((2, ZH, N, CH), BF16),
            pltpu.VMEM((2, ZH, N, CH), BF16),
            dma((17,)),
            dma((N,)), dma((N,)), dma((N,)), dma((N,)), dma((N,)), dma((N,)), dma((N,)), dma((N,)),
            dma((2, 26)),
        ],
        compiler_params=pltpu.CompilerParams(
            collective_id=0, has_side_effects=True, vmem_limit_bytes=59 << 20
        ),
        name="exchange",
    )(
        page_table.T, dest_instance.reshape(1, N), dest_slot.reshape(1, N), lengths.reshape(1, N),
        query_one, key_one.reshape(N, HD), value_one.reshape(N, HD),
        query_two, key_two.reshape(N, HD), value_two.reshape(N, HD),
        key_pages.reshape(pool, PAGE, HD), value_pages.reshape(pool, PAGE, HD), out_weight,
    )
    out1, out2, key_cache, value_cache = pl.pallas_call(
        place_kernel,
        out_shape=(
            jax.ShapeDtypeStruct((N, columns), BF16),
            jax.ShapeDtypeStruct((N, columns), BF16),
            jax.ShapeDtypeStruct((N, 2, HALF, HD), BF16),
            jax.ShapeDtypeStruct((N, 2, HALF, HD), BF16),
        ),
        in_specs=[smem, vmem, vmem, vmem],
        out_specs=(hbm, hbm, hbm, hbm),
        scratch_shapes=[dma((2 + 2 * TP,))],
        compiler_params=pltpu.CompilerParams(vmem_limit_bytes=48 << 20),
        name="place",
    )(hdr, *(pltpu.with_memory_space_constraint(a, pltpu.VMEM) for a in (moved, part1, part2)))
    shape = (N * PR, 1, PAGE, HD)
    return out1, out2, key_cache.reshape(shape), value_cache.reshape(shape)


def solution(mesh):
    return jax.shard_map(
        shards,
        mesh=mesh,
        in_specs=(
            P("inst", "tp", None),
            P("inst", "tp", None),
            P("inst", "tp", None),
            P("inst", "tp", None, None),
            P("inst", "tp", None, None),
            P("inst", None),
            P("inst"),
            P("inst"),
            P("inst"),
            P("inst", "tp", None),
            P("inst", "tp", None),
            P("inst", "tp", None),
            P("tp", None),
        ),
        out_specs=(
            P("inst", None),
            P("inst", None),
            P("inst", "tp", None, None),
            P("inst", "tp", None, None),
        ),
        check_vma=False,
    )
```

```python
import jax
import jax.numpy as jnp
from jax import lax
from jax.experimental import pallas as pl
from jax.experimental.pallas import tpu as pltpu
from jax.sharding import PartitionSpec as P

MESH = pl.DeviceIdType.MESH
NEG = -1e30
N = 32
TP = 8
ZH = 4
PR = 4
PAGE = 64
SPAN = PR * PAGE
HD = 128
G = 8
CH = 512
QUARTERS = 4
HALF = SPAN // 2
BATCH = 8
PIECES = N * QUARTERS
WINDOW = 14
F32 = jnp.float32
BF16 = jnp.bfloat16


def iota(shape, dim):
    return lax.broadcasted_iota(jnp.int32, shape, dim)


def attend(queries, keys, values, counts):
    scores = [
        lax.dot_general(q, k, (((1,), (1,)), ((), ())), preferred_element_type=F32)
        for q, k in zip(queries, keys)
    ]
    live = jnp.concatenate([iota((G, SPAN), 1) < n for n in counts], axis=0)
    scores = jnp.concatenate(scores, axis=0) * HD ** (-0.5)
    scores = jnp.where(live, scores, NEG)
    top = jnp.max(scores, axis=-1, keepdims=True)
    expo = jnp.where(live, jnp.exp(scores - top), 0.0)
    weights = (expo / jnp.sum(expo, axis=-1, keepdims=True)).astype(BF16)
    return [
        jnp.dot(weights[i * G : (i + 1) * G], v, preferred_element_type=F32)
        for i, v in enumerate(values)
    ]


def put_token(page, token, first_row, position):
    return jnp.where(iota(page.shape, 0) + first_row == position, token, page)


def exchange_kernel(
    pt_hbm, dest_hbm, slot_hbm, len_hbm, q1_hbm, k1_hbm, v1_hbm, q2_hbm, k2_hbm, v2_hbm, kp, vp, w_hbm,
    moved, hdr_rs, out1, out2,
    pt, dest_s, len_s, dest_v, slot_v, len_v, q1, q2, tok_b, tok, kpv, vpv, w, send, tab_v, tab_s, hdr_s, hdr_r, rep_s, rep_r, o1, os, orr, lhs,
    own, pa_s, pa_r, pb_s, pb_r,
    lsem, hs, hr, rs, rr, ss, sr, bs, br, psem,
):
    me, tp = lax.axis_index("inst"), lax.axis_index("tp")
    x, y, zl = me % 4, (me // 4) % 4, me // 16
    core, zh = tp % 2, tp // 2

    def load(src, dst, i):
        return pltpu.make_async_copy(src, dst, lsem.at[i])

    small = [
        load(src, dst, 5 + i)
        for i, (src, dst) in enumerate((
            (dest_hbm, dest_v), (slot_hbm, slot_v), (len_hbm, len_v), (pt_hbm, pt),
            (dest_hbm, dest_s), (len_hbm, len_s),
            (k1_hbm, tok_b.at[0]), (v1_hbm, tok_b.at[1]), (k2_hbm, tok_b.at[2]), (v2_hbm, tok_b.at[3]),
            (q1_hbm, q1), (q2_hbm, q2),
        ))
    ]
    for copy in small[:8]:
        copy.start()
    load(kp, kpv, 0).start()
    load(vp, vpv, 1).start()
    for copy in small[8:]:
        copy.start()
    load(w_hbm, w, 2).start()

    barrier = pltpu.get_barrier_semaphore()

    def greet_inst(i, c):
        pl.semaphore_signal(barrier, inc=1, device_id={"inst": (me + i) % N}, device_id_type=MESH)
        return c

    def greet_tp(i, c):
        pl.semaphore_signal(barrier, inc=1, device_id={"tp": (tp + i) % TP}, device_id_type=MESH)
        return c

    lax.fori_loop(1, N, greet_inst, 0)
    lax.fori_loop(1, TP, greet_tp, 0)

    for copy in small[:8]:
        copy.wait()

    here = dest_v[...] == iota((N, N), 0)
    row = jnp.max(jnp.where(here, iota((N, N), 1), 0), axis=1, keepdims=True)
    length = jnp.max(jnp.where(here, len_v[...], 0), axis=1, keepdims=True)
    slot = jnp.max(jnp.where(here, slot_v[...], 0), axis=1, keepdims=True)
    lane = iota((N, 128), 1)
    tab_v[...] = jnp.where(lane < 32, row, jnp.where(lane < 64, length, slot))
    to_scalar = load(tab_v, tab_s, 3)
    to_scalar.start()
    to_scalar.wait()

    def header(t, c):
        hdr_s[t] = jnp.where(iota((1, 128), 1) < 64, tab_s[t, 64], tab_s[t, 32])
        return c

    lax.fori_loop(0, N, header, 0)

    def remote(src, dst, send_sem, recv_sem, device):
        return pltpu.make_async_remote_copy(
            src_ref=src, dst_ref=dst, send_sem=send_sem, recv_sem=recv_sem,
            device_id=device, device_id_type=MESH,
        )

    def each_other(body):
        def step(i, c):
            body((me + i) % N)
            return c

        lax.fori_loop(1, N, step, 0)

    def send_header(t):
        return remote(hdr_s.at[t], hdr_r.at[me], hs.at[t], hr.at[me], {"inst": t})

    def wait_header(t):
        return remote(hdr_s.at[t], hdr_r.at[t], hs.at[t], hr.at[t], {"inst": t})

    pl.semaphore_wait(barrier, N + TP - 2)
    each_other(lambda t: send_header(t).start())
    hdr_r[me] = hdr_s[me]

    def offset(k):
        i, j = k % 4, k // 4
        dx, dy, dz = i, (i + j) % 4, (i // 2 + j // 4) % 2
        return dx, dy, dz

    def target(k, sign):
        dx, dy, dz = offset(k)
        turn = sign * (1 - 2 * core)
        return (((zl + dz) % 2) * 4 + (y + 4 + turn * dy) % 4) * 4 + (x + 4 + turn * dx) % 4

    def gather(t):
        r, n = tab_s[t, 0], tab_s[t, 32]
        for which, pages in enumerate((kpv, vpv)):
            token = tok[which, pl.ds(r, 1), :].astype(BF16)
            for p in range(PR):
                page = put_token(pages[pt[p, r]], token, p * PAGE, n)
                at = p * PAGE % HALF
                send[t, which * 2 + p * PAGE // HALF, at : at + PAGE] = page

    def gathers(lo, hi):
        def step(k, c):
            gather(target(k, 1))
            return c

        lax.fori_loop(lo, hi, step, 0)

    def piece(v):
        k, quarter = v // (BATCH * QUARTERS) * BATCH + v % BATCH, v // BATCH % QUARTERS
        t = target(k, 1)
        return k, remote(send.at[t, quarter], moved.at[me, quarter], bs.at[v % 16], br.at[me], {"inst": t})

    def piece_start(v):
        k, copy = piece(v)

        @pl.when(k != 0)
        def _():
            copy.start()

    def piece_sent(v):
        k, copy = piece(v)

        @pl.when(k != 0)
        def _():
            copy.wait_send()

    def pumps(lo, hi):
        def step(v, c):
            piece_sent(v - WINDOW)
            piece_start(v)
            return c

        lax.fori_loop(lo, hi, step, 0)

    def cache_of(ref, t):
        return [ref[t, 2 * which : 2 * which + 2].reshape(SPAN, HD) for which in range(2)]

    def block_in(k):
        s = target(k, -1)
        return remote(send.at[s], moved.at[s], bs.at[0], br.at[s], {"inst": s}), s

    for copy in small[8:]:
        copy.wait()
    tok[...] = tok_b[...].astype(F32)
    load(kp, kpv, 0).wait()
    load(vp, vpv, 1).wait()
    gathers(0, BATCH)

    def begin(v, c):
        piece_start(v)
        return c

    lax.fori_loop(0, WINDOW, begin, 0)
    gathers(BATCH, 2 * BATCH)
    pumps(14, 16)
    gathers(2 * BATCH, N)
    pumps(16, 18)

    def attend_one(g, c):
        rows = [g * BATCH + i for i in range(BATCH)]
        caches = [cache_of(send, dest_s[0, r]) for r in rows]
        res = attend(
            [q1[r] for r in rows], [k for k, _ in caches], [v for _, v in caches],
            [len_s[0, r] + 1 for r in rows],
        )
        for r, one in zip(rows, res):
            o1[pl.ds(pl.multiple_of(r * G, G), G), :] = one
        pumps(18 + 2 * g, 20 + 2 * g)
        return c

    lax.fori_loop(0, N // BATCH, attend_one, 0)

    each_other(lambda t: wait_header(t).wait())
    fetch = load(hdr_r, hdr_rs, 4)
    fetch.start()
    fetch.wait()

    def reply(s):
        j = hdr_rs[s, 0, 0]
        token = jnp.where(iota((G, HD), 0) == 0, tok[2, pl.ds(j, 1), :], tok[3, pl.ds(j, 1), :])
        rep_s[s] = jnp.concatenate([q2[j].astype(F32), token], axis=0).astype(BF16)

    def reply_to(s):
        reply(s)
        remote(rep_s.at[s], rep_r.at[me], rs.at[s], rr.at[me], {"inst": s}).start()

    each_other(reply_to)
    reply(me)
    rep_r[me] = rep_s[me]
    pumps(26, 32)

    def project(side, chunk):
        at = pl.multiple_of(side * (ZH * CH) + chunk * CH, CH)
        return jnp.dot(lhs[...], w[:, pl.ds(at, CH)], preferred_element_type=F32)

    def heads_side_by_side(ref):
        parts = [ref[pl.ds(h, N, stride=G), :] for h in range(G)]
        return jnp.concatenate(parts, axis=1).astype(BF16)

    other = {"tp": zh * 2 + 1 - core}

    def sum_a(i, v):
        def away(h, c):
            pa_s[i, h] = project(1 - core, h).astype(BF16)
            pumps(v + h, v + h + 1)
            return c

        lax.fori_loop(0, ZH, away, 0)
        remote(pa_s.at[i], pa_r.at[i], psem.at[i, 0], psem.at[i, 1], other).start()

        def keep(h, c):
            own[i, h] = project(core, h)
            pumps(v + ZH + h, v + ZH + h + 1)
            return c

        lax.fori_loop(0, ZH, keep, 0)

    def part_b(i, d):
        h = (zh + d) % ZH
        return remote(pb_s.at[i, h], pb_r.at[i, zh], psem.at[i, 2 + d], psem.at[i, 6 + zh], {"tp": h * 2 + core}), h

    def sum_b(i):
        remote(pa_s.at[i], pa_r.at[i], psem.at[i, 0], psem.at[i, 1], other).wait()
        for h in range(ZH):
            both = own[i, h] + pa_r[i, h].astype(F32)
            own[i, h] = both
            pb_s[i, h] = both.astype(BF16)
        for d in range(1, ZH):
            part_b(i, d)[0].start()

    outs = (out1, out2)

    def chunk_to(i, h, device, send_at, recv_at):
        at = core * ZH + h
        return remote(outs[i].at[at], outs[i].at[at], psem.at[i, send_at], psem.at[i, recv_at], device)

    def sum_c(i):
        total = own[i, zh]
        for d in range(1, ZH):
            part, h = part_b(i, d)
            part.wait_send()
            remote(pb_s.at[i, h], pb_r.at[i, h], psem.at[i, 2 + d], psem.at[i, 6 + h], {"tp": h * 2 + core}).wait_recv()
            total = total + pb_r[i, h].astype(F32)
        outs[i][core * ZH + zh] = total.astype(BF16)
        for d in range(1, ZH):
            chunk_to(i, zh, {"tp": ((zh + d) % ZH) * 2 + core}, 10 + d, 14 + zh).start()
        chunk_to(i, zh, other, 18 + zh, 22 + zh).start()

    def sum_d(i):
        for d in range(1, ZH):
            h = (zh + d) % ZH
            chunk_to(i, h, {"tp": h * 2 + core}, 10 + d, 14 + h).wait()
            chunk_to(i, h, other, 18 + h, 22 + h).start()

    def sum_end(i):
        for h in range(ZH):
            at = (1 - core) * ZH + h
            chunk_to(i, h, other, 18 + h, 22 + h).wait_send()
            remote(outs[i].at[at], outs[i].at[at], psem.at[i, 18 + h], psem.at[i, 22 + h], other).wait_recv()

    load(w_hbm, w, 2).wait()
    lhs[...] = heads_side_by_side(o1)
    sum_a(0, 32)
    pumps(40, 44)
    sum_b(0)
    pumps(44, 54)

    each_other(lambda t: remote(rep_s.at[t], rep_r.at[t], rs.at[t], rr.at[t], {"inst": t}).wait())

    def result_out(t):
        return remote(os.at[t], orr.at[me], ss.at[t], sr.at[me], {"inst": t})

    def result_in(s):
        return remote(os.at[s], orr.at[s], ss.at[s], sr.at[s], {"inst": s})

    def attend_two(g, v, keep):
        ts = [target(g * BATCH + i, 1) for i in range(BATCH)]
        tiles = [rep_r[t].astype(F32) for t in ts]
        at = [tab_s[t, 32] + 1 for t in ts]
        caches = [
            [put_token(c, m[G + i : G + i + 1].astype(BF16), 0, n) for i, c in enumerate(cache_of(send, t))]
            for t, m, n in zip(ts, tiles, at)
        ]
        if keep:
            for t, cache in zip(ts, caches):
                for which, c in enumerate(cache):
                    send[t, 2 * which : 2 * which + 2] = c.reshape(2, HALF, HD)
        res = attend(
            [m[:G].astype(BF16) for m in tiles], [k for k, _ in caches], [v for _, v in caches],
            [n + 1 for n in at],
        )
        for t, one in zip(ts, res):
            os[t] = one.astype(BF16)
        for i, t in enumerate(ts):

            @pl.when(g * BATCH + i != 0)
            def _():
                result_out(t).start()

        pumps(v, v + 2)

    def late_blocks(g, c):
        attend_two(g, 54 + 2 * (g - 2), True)
        return c

    def early_blocks(g, c):
        attend_two(g, 58 + 2 * g, False)
        return c

    lax.fori_loop(2, 4, late_blocks, 0)
    lax.fori_loop(0, 2, early_blocks, 0)
    orr[me] = os[me]
    pumps(62, 70)
    sum_c(0)
    pumps(70, 80)

    each_other(lambda s: result_in(s).wait())
    o1[...] = orr[...].astype(F32).reshape(N * G, HD)

    def slot_row(s, acc):
        return jnp.where(iota((1, 128), 1) == s, hdr_rs[s, 0, 0], acc)

    slots = lax.fori_loop(0, N, slot_row, jnp.zeros((1, 128), jnp.int32))
    pick = jnp.where(slots[:, :N] == iota((N, N), 0), 1.0, 0.0).astype(BF16)
    lhs[...] = jnp.dot(pick, heads_side_by_side(o1), preferred_element_type=F32).astype(BF16)
    sum_a(1, 80)
    sum_d(0)

    def finish(s):
        n, j = hdr_rs[s, 0, 64] + 1, hdr_rs[s, 0, 0]
        for which, page in enumerate(cache_of(moved, s)):
            token = tok[2 + which, pl.ds(j, 1), :].astype(BF16)
            moved[s, 2 * which : 2 * which + 2] = put_token(page, token, 0, n).reshape(2, HALF, HD)

    def arrive(k, c):
        copy, s = block_in(k)
        copy.wait_recv()
        finish(s)
        return c

    def arrive_late(k, c):
        copy, _ = block_in(k)
        copy.wait_recv()
        return c

    moved[me] = send[me]
    finish(me)
    lax.fori_loop(1, BATCH, arrive, 0)
    pumps(88, 92)
    sum_b(1)
    pumps(92, 108)
    sum_end(0)
    sum_c(1)
    lax.fori_loop(BATCH, 2 * BATCH, arrive, 0)
    pumps(108, PIECES)
    sum_d(1)

    def sent(v, c):
        piece_sent(v)
        return c

    lax.fori_loop(PIECES - WINDOW, PIECES, sent, 0)
    lax.fori_loop(2 * BATCH, N, arrive_late, 0)
    sum_end(1)


def place_kernel(hdr, moved, part1, part2, out1, out2, key_cache, value_cache, sems):
    caches = (key_cache, value_cache)
    columns = [
        pltpu.make_async_copy(part.at[c], out.at[:, pl.ds(c * CH, CH)], sems.at[2 + i * TP + c])
        for i, (part, out) in enumerate(((part1, out1), (part2, out2)))
        for c in range(TP)
    ]

    def put(s, c):
        for which, cache in enumerate(caches):
            half = moved.at[s, pl.ds(2 * which, 2)]
            pltpu.make_async_copy(half, cache.at[hdr[s, 0, 0]], sems.at[which]).start()
        return c

    lax.fori_loop(0, N, put, 0, unroll=4)
    for copy in columns:
        copy.start()
    for copy in columns:
        copy.wait()
    for which, cache in enumerate(caches):
        pltpu.make_async_copy(moved.at[:, pl.ds(2 * which, 2)], cache, sems.at[which]).wait()


def shards(
    query_one, key_one, value_one, key_pages, value_pages, page_table, lengths,
    dest_instance, dest_slot, query_two, key_two, value_two, out_weight,
):
    vmem = pl.BlockSpec(memory_space=pltpu.VMEM)
    smem = pl.BlockSpec(memory_space=pltpu.SMEM)
    hbm = pl.BlockSpec(memory_space=pltpu.HBM)
    columns = out_weight.shape[1]
    pool = key_pages.shape[0]
    dma = pltpu.SemaphoreType.DMA
    moved, hdr, part1, part2 = pl.pallas_call(
        exchange_kernel,
        out_shape=(
            pltpu.VMEM((N, QUARTERS, HALF, HD), BF16),
            pltpu.SMEM((N, 1, 128), jnp.int32),
            pltpu.VMEM((TP, N, CH), BF16),
            pltpu.VMEM((TP, N, CH), BF16),
        ),
        in_specs=[hbm] * 13,
        out_specs=(vmem, smem, vmem, vmem),
        scratch_shapes=[
            pltpu.SMEM((PR, N), jnp.int32),
            pltpu.SMEM((1, N), jnp.int32),
            pltpu.SMEM((1, N), jnp.int32),
            pltpu.VMEM((1, N), jnp.int32),
            pltpu.VMEM((1, N), jnp.int32),
            pltpu.VMEM((1, N), jnp.int32),
            pltpu.VMEM((N, G, HD), BF16),
            pltpu.VMEM((N, G, HD), BF16),
            pltpu.VMEM((4, N, HD), BF16),
            pltpu.VMEM((4, N, HD), F32),
            pltpu.VMEM((pool, PAGE, HD), BF16),
            pltpu.VMEM((pool, PAGE, HD), BF16),
            pltpu.VMEM((G * HD, columns), BF16),
            pltpu.VMEM((N, QUARTERS, HALF, HD), BF16),
            pltpu.VMEM((N, 128), jnp.int32),
            pltpu.SMEM((N, 128), jnp.int32),
            pltpu.VMEM((N, 1, 128), jnp.int32),
            pltpu.VMEM((N, 1, 128), jnp.int32),
            pltpu.VMEM((N, 2 * G, HD), BF16),
            pltpu.VMEM((N, 2 * G, HD), BF16),
            pltpu.VMEM((N * G, HD), F32),
            pltpu.VMEM((N, G, HD), BF16),
            pltpu.VMEM((N, G, HD), BF16),
            pltpu.VMEM((N, G * HD), BF16),
            pltpu.VMEM((2, ZH, N, CH), F32),
            pltpu.VMEM((2, ZH, N, CH), BF16),
            pltpu.VMEM((2, ZH, N, CH), BF16),
            pltpu.VMEM((2, ZH, N, CH), BF16),
            pltpu.VMEM((2, ZH, N, CH), BF16),
            dma((17,)),
            dma((N,)), dma((N,)), dma((N,)), dma((N,)), dma((N,)), dma((N,)), dma((N,)), dma((N,)),
            dma((2, 26)),
        ],
        compiler_params=pltpu.CompilerParams(
            collective_id=0, has_side_effects=True, vmem_limit_bytes=59 << 20
        ),
        name="exchange",
    )(
        page_table.T, dest_instance.reshape(1, N), dest_slot.reshape(1, N), lengths.reshape(1, N),
        query_one, key_one.reshape(N, HD), value_one.reshape(N, HD),
        query_two, key_two.reshape(N, HD), value_two.reshape(N, HD),
        key_pages.reshape(pool, PAGE, HD), value_pages.reshape(pool, PAGE, HD), out_weight,
    )
    out1, out2, key_cache, value_cache = pl.pallas_call(
        place_kernel,
        out_shape=(
            jax.ShapeDtypeStruct((N, columns), BF16),
            jax.ShapeDtypeStruct((N, columns), BF16),
            jax.ShapeDtypeStruct((N, 2, HALF, HD), BF16),
            jax.ShapeDtypeStruct((N, 2, HALF, HD), BF16),
        ),
        in_specs=[smem, vmem, vmem, vmem],
        out_specs=(hbm, hbm, hbm, hbm),
        scratch_shapes=[dma((2 + 2 * TP,))],
        compiler_params=pltpu.CompilerParams(vmem_limit_bytes=48 << 20),
        name="place",
    )(pltpu.with_memory_space_constraint(hdr, pltpu.SMEM), *(pltpu.with_memory_space_constraint(a, pltpu.VMEM) for a in (moved, part1, part2)))
    shape = (N * PR, 1, PAGE, HD)
    return out1, out2, key_cache.reshape(shape), value_cache.reshape(shape)


def solution(mesh):
    return jax.shard_map(
        shards,
        mesh=mesh,
        in_specs=(
            P("inst", "tp", None),
            P("inst", "tp", None),
            P("inst", "tp", None),
            P("inst", "tp", None, None),
            P("inst", "tp", None, None),
            P("inst", None),
            P("inst"),
            P("inst"),
            P("inst"),
            P("inst", "tp", None),
            P("inst", "tp", None),
            P("inst", "tp", None),
            P("tp", None),
        ),
        out_specs=(
            P("inst", None),
            P("inst", None),
            P("inst", "tp", None, None),
            P("inst", "tp", None, None),
        ),
        check_vma=False,
    )
```
